1024 devices in a mesh: grp: 16 (over x, y), loc: 64 (over z, core).
Axes of the slice: x: 4, y: 4, z: 32, core: 2. Of those that a mesh axis runs over, the one named last changes fastest.
Arguments:
- tokens: bfloat16 [4096, 7168], P('loc', 'grp'), may hold values from -6 to 6
- expert_ids: int32 [4096, 8], P('loc'), may hold values from 0 to 63, all different within a row; in each aligned block of 64 rows (0 to 63, 64 to 127, ...) at most 16 rows name the same one
- route_weight: float32 [4096, 8], P('loc'), may hold values from 0.1 to 1
- w_gate: bfloat16 [64, 7168, 1024], P('loc', 'grp'), may hold values from -0.0625 to 0.0625
- w_up: bfloat16 [64, 7168, 1024], P('loc', 'grp'), may hold values from -0.0625 to 0.0625
- w_down: bfloat16 [64, 1024, 7168], P('loc', None, 'grp'), may hold values from -0.1875 to 0.1875
Outputs:
- mixed: bfloat16 [4096, 7168], P('loc', 'grp')
The draws below stay inside these ranges and needn't reach their ends.
Inputs may be any that keep to these rules, and one draw needn't show every extreme that they name: `expert_ids`: each row names 8 different experts. Among the rows of one index of loc no expert is named more than 16 times, a bound that some block reaches.
All inputs are finite; a program needn't handle non-finite values.
Results may differ from the reference program's by a relative error of at most 0.03.
Values may be sent and summed in bfloat16 or wider, within the bound.
A program may use at most 32 MiB of HBM per device.

```python
import math
import jax
import jax.numpy as jnp
import numpy as np
from jax import lax

D = 7168
FF = 1024
TOPK = 8
TOK_DEV = 64
TOKENS = 4096
EXPERTS = 64
CAP = 16
N_GRP = 16


def block_levels(stream_key, dims, split, smallest, largest):
    gain, own = 1.0, jax.random.fold_in(stream_key, 6)
    for axis_at, blocks in split:
        steps = jnp.exp(jax.random.uniform(jax.random.fold_in(own, axis_at), (blocks,), jnp.float32, smallest / len(split), largest / len(split)))
        gain = gain * jnp.repeat(steps, dims[axis_at] // blocks).reshape([-1 if axis == axis_at else 1 for axis in range(len(dims))])
    return gain


def routed_block(key, own, number, rows, number_of, top, limit, skew):
    order = jax.random.permutation(key, number_of)
    crowded, usual = shares(number_of, rows * top, limit, skew, True), shares(number_of, rows * top, limit, skew, False)
    places = jnp.arange(number_of)

    def named(sizes, offset_by):
        used = int((sizes > 0).sum())
        fixed = max(1, used // 4)
        passed = fixed + (places - fixed + offset_by * (used - fixed)) % max(1, number_of - fixed)
        return jnp.zeros((number_of,), jnp.int32).at[order[jnp.where(places < fixed, places, passed)]].set(jnp.asarray(sizes, jnp.int32))

    sizes = jnp.where(number % 4 == 0, named(crowded, number // 4), named(usual, number - number // 4 - 1))
    mixed = jax.random.permutation(jax.random.fold_in(own, 3), number_of)
    source_of, receiver = mixed[0:number_of // 2 * 2:2], mixed[1:number_of // 2 * 2:2]
    room = jnp.minimum(sizes[source_of] - 1, limit - sizes[receiver]) // 2
    room = jnp.where((source_of == order[0]) | (receiver == order[0]) | (sizes[receiver] == 0), 0, jnp.maximum(room, 0))
    passed = jax.random.randint(jax.random.fold_in(own, 4), (number_of // 2,), 0, 1 << 20) % (room + 1)
    sizes = sizes.at[source_of].add(-passed).at[receiver].add(passed)
    members = jnp.searchsorted(jnp.cumsum(sizes), jnp.arange(rows * top), side="right").astype(jnp.int32)
    listing = members.reshape(top, rows).T
    listing = listing[jax.random.permutation(jax.random.fold_in(own, 1), rows)]
    offset_by = jax.random.randint(jax.random.fold_in(own, 2), (rows, 1), 0, top)
    return jnp.take_along_axis(listing, (jnp.arange(top)[None, :] + offset_by) % top, axis=1)


def shares(count, total, reach, lean, full):
    loads = [(1 << 20) // math.isqrt(rank ** lean) + 1 for rank in range(1, count + 1)]
    largest = reach if full else min(reach, max(-(-total // count), total * loads[0] // sum(loads)))
    least = 1 if total - largest >= count - 1 else 0
    holding, surplus = [largest] + [least] * (count - 1), total - largest - least * (count - 1)
    while surplus > 0:
        movable = [i for i in range(1, count) if holding[i] < largest] or [i for i in range(1, count) if holding[i] < reach]
        pool, left = sum([loads[i] for i in movable]), surplus
        for i in movable:
            extra = min(reach - holding[i], max(1, left * loads[i] // pool), surplus)
            holding[i] = holding[i] + extra
            surplus = surplus - extra
    return np.array(holding)


def centred(rng, extent, width, most, shards=(), kind=jnp.bfloat16):
    result = jax.random.normal(rng, extent, jnp.float32) * width
    if len(shards) > 0:
        result = block_levels(rng, extent, shards, -0.22, 0.18) * result
    return jnp.clip(result, min=-most, max=most).astype(kind)


def setup_inputs(seed: int = 0) -> dict:
    streams_of = jax.random.split(jax.random.key(seed), 7)
    tokens = centred(streams_of[0], (TOKENS, D), 1.0, 6.0, ((0, 64), (1, 16)))
    expert_ids_keys = jax.random.split(jax.random.fold_in(streams_of[1], 1), TOKENS // TOK_DEV)
    expert_ids_turns = jax.random.permutation(jax.random.fold_in(streams_of[1], 3), TOKENS // TOK_DEV)
    expert_ids = jax.vmap(lambda own, number: routed_block(jax.random.fold_in(streams_of[1], 2), own, number, TOK_DEV, EXPERTS, TOPK, CAP, 2))(expert_ids_keys, expert_ids_turns).reshape((TOKENS, TOPK))
    route_weight = jnp.clip(jnp.exp(math.log(1.0) - 2.3025851 * jax.random.uniform(streams_of[2], (TOKENS, TOPK), jnp.float32) ** block_levels(streams_of[2], (TOKENS, TOPK), ((0, 64),), -0.2, 0.2)), 0.1, 1.0)
    w_gate = centred(streams_of[3], (EXPERTS, D, FF), D ** -0.5, 0.0625, ((0, 64), (1, 16)))
    w_up = centred(streams_of[4], (EXPERTS, D, FF), D ** -0.5, 0.0625, ((0, 64), (1, 16)))
    w_down = centred(streams_of[5], (EXPERTS, FF, D), FF ** -0.5, 0.1875, ((0, 64), (2, 16)))
    return {"tokens": tokens, "expert_ids": expert_ids, "route_weight": route_weight, "w_gate": w_gate, "w_up": w_up, "w_down": w_down}


def reference(tokens, expert_ids, route_weight, w_gate, w_up, w_down):
    token_total = tokens.shape[0]
    expert_count = w_gate.shape[0]
    block_count = token_total // TOK_DEV
    slot_rows = block_count * CAP
    flat_ids = expert_ids.reshape(block_count, TOK_DEV * TOPK)
    expert_hits = (flat_ids[:, :, None] == jnp.arange(expert_count, dtype=jnp.int32)[None, None, :]).astype(jnp.int32)
    position = jnp.sum(jnp.cumsum(expert_hits, axis=1) * expert_hits, axis=2) - 1
    block_index = jnp.arange(block_count, dtype=jnp.int32)[:, None]
    slot = (block_index * CAP + position).astype(jnp.int32)
    token_index = (block_index * TOK_DEV + jnp.arange(TOK_DEV * TOPK, dtype=jnp.int32)[None, :] // TOPK).astype(jnp.int32)
    table = jnp.full((expert_count, slot_rows), token_total, jnp.int32)
    table = table.at[flat_ids.reshape(-1), slot.reshape(-1)].set(token_index.reshape(-1))
    padded = jnp.concatenate([tokens, jnp.zeros((1, D), jnp.bfloat16)], axis=0)
    block_width = D // N_GRP

    def one_expert(pieces):
        row_table, gate_mat, up_mat, down_mat = pieces
        gathered = padded[row_table].astype(jnp.float32).reshape(slot_rows, N_GRP, block_width)

        def block_sum(weight):
            blocks = weight.astype(jnp.float32).reshape(N_GRP, block_width, FF)
            part = jnp.einsum("rgd,gdf->grf", gathered, blocks, precision=lax.Precision.HIGHEST)
            part = lax.optimization_barrier(part.astype(jnp.bfloat16))
            return jnp.sum(part.astype(jnp.float32), axis=0)

        gate = block_sum(gate_mat)
        upper = block_sum(up_mat)
        hidden = (jax.nn.silu(gate) * upper).astype(jnp.bfloat16)
        return jnp.dot(hidden, down_mat, preferred_element_type=jnp.float32).astype(jnp.bfloat16)

    outputs = lax.map(one_expert, (table, w_gate, w_up, w_down))
    picked = outputs[flat_ids.reshape(-1), slot.reshape(-1)].astype(jnp.float32)
    picked = picked.reshape(token_total, TOPK, D)
    mixed = jnp.sum(picked * route_weight[:, :, None], axis=1)
    return mixed.astype(jnp.bfloat16)
```

```python
import functools

import jax
import jax.numpy as jnp
from jax import lax
from jax.experimental import pallas as pl
from jax.experimental.pallas import tpu as pltpu
from jax.sharding import PartitionSpec as P

MESH = pl.DeviceIdType.MESH
BF16 = jnp.bfloat16
F32 = jnp.float32
SIDE = 4
META = 64


def remote(src, dst, send_sem, recv_sem, device):
    return pltpu.make_async_remote_copy(
        src_ref=src,
        dst_ref=dst,
        send_sem=send_sem,
        recv_sem=recv_sem,
        device_id=device,
        device_id_type=MESH,
    )


class RingSum:
    def __init__(self, source, place, right, left, recv, send, send_sem, recv_sem):
        self.source, self.place, self.right, self.left = source, place, right, left
        self.recv, self.send, self.send_sem, self.recv_sem = recv, send, send_sem, recv_sem

    def copy(self, c, kind):
        after, before = lax.rem(self.place + 1, SIDE), lax.rem(self.place + 3, SIDE)
        across = lax.rem(self.place + 2, SIDE)
        src = (
            lambda: self.source(c, 0, across),
            lambda: self.source(c, 1, after),
            lambda: self.source(c, 1, across),
            lambda: self.source(c, 0, before),
            lambda: self.send.at[c, 0],
            lambda: self.send.at[c, 1],
        )[kind]()
        to = (self.right, self.right, self.left, self.left, self.right, self.left)[kind]
        return remote(
            src, self.recv.at[c, kind], self.send_sem.at[c, kind], self.recv_sem.at[c, kind], to
        )

    def first(self, c):
        for kind in range(4):
            self.copy(c, kind).start()

    def second(self, c):
        after, before = lax.rem(self.place + 1, SIDE), lax.rem(self.place + 3, SIDE)
        self.copy(c, 0).wait_recv()
        total = self.source(c, 0, after)[...].astype(F32) + self.recv[c, 0].astype(F32)
        self.send[c, 0] = total.astype(BF16)
        self.copy(c, 4).start()
        self.copy(c, 2).wait_recv()
        total = self.source(c, 1, before)[...].astype(F32) + self.recv[c, 2].astype(F32)
        self.send[c, 1] = total.astype(BF16)
        self.copy(c, 5).start()

    def last(self, c):
        for kind in (1, 3, 4, 5):
            self.copy(c, kind).wait_recv()
        gate = self.source(c, 0, self.place)[...].astype(F32) + self.recv[c, 3].astype(F32)
        gate = gate + self.recv[c, 4].astype(F32)
        up = self.source(c, 1, self.place)[...].astype(F32) + self.recv[c, 1].astype(F32)
        up = up + self.recv[c, 5].astype(F32)
        return gate, up

    def finish(self, c):
        for kind in range(6):
            self.copy(c, kind).wait_send()


class RingGather:
    def __init__(self, piece, half, place, right, left, send_sem, recv_sem):
        self.piece, self.half, self.place, self.right, self.left = piece, half, place, right, left
        self.send_sem, self.recv_sem = send_sem, recv_sem

    def copy(self, c, kind, receiving=False):
        if receiving:
            at = lax.rem(self.place + (3, 1, 2, 2)[kind], SIDE)
        else:
            at = lax.rem(self.place + (0, 0, 3, 1)[kind], SIDE)
        ref = self.piece(c, at) if kind < 2 else self.half(c, at, kind - 2)
        to = (self.right, self.left, self.right, self.left)[kind]
        return remote(ref, ref, self.send_sem.at[c, kind], self.recv_sem.at[c, kind], to)

    def first(self, c):
        self.copy(c, 0).start()
        self.copy(c, 1).start()

    def second(self, c):
        self.copy(c, 0, True).wait_recv()
        self.copy(c, 2).start()
        self.copy(c, 1, True).wait_recv()
        self.copy(c, 3).start()

    def last(self, c):
        self.copy(c, 2, True).wait_recv()
        self.copy(c, 3, True).wait_recv()

    def finish(self, c):
        for kind in range(4):
            self.copy(c, kind).wait_send()


def kernel(
    steps, chunks, blk, wg_hbm, wu_hbm, wd_hbm, out_ref,
    tr, tl, wm, xb, xs, wg, wu, wd, pa, pb,
    ra1, sa1, rb1, sb1, qa, qb, ra2, sa2, rb2, sb2, ha, hb,
    ob, os_, or_, zr, szr, zl, szl,
    w_sem, tr_s, tr_r, tl_s, tl_r, x_s, x_r, o_s, o_r,
    a1_s, a1_r, b1_s, b1_r, a2_s, a2_r, b2_s, b2_r,
    ga1_s, ga1_r, gb1_s, gb1_r, ga2_s, ga2_r, gb2_s, gb2_r,
    zr_s, zr_r, zl_s, zl_r,
):
    features = wd.shape[1]
    grp, loc = lax.axis_index("grp"), lax.axis_index("loc")
    depth = lax.axis_size("loc") // 2
    x, y = grp // SIDE, lax.rem(grp, SIDE)
    z, core = loc // 2, lax.rem(loc, 2)
    x_right = (lax.rem(x + 1, SIDE) * SIDE + y, loc)
    x_left = (lax.rem(x + 3, SIDE) * SIDE + y, loc)
    y_right = (x * SIDE + lax.rem(y + 1, SIDE), loc)
    y_left = (x * SIDE + lax.rem(y + 3, SIDE), loc)
    z_right = (grp, lax.rem(z + 1, depth) * 2 + core)
    z_left = (grp, lax.rem(z + depth - 1, depth) * 2 + core)
    sibling = (grp, z * 2 + 1 - core)

    weight_copies = [
        pltpu.make_async_copy(wg_hbm.at[0], wg.at[pl.ds(META, features)], w_sem.at[0]),
        pltpu.make_async_copy(wu_hbm.at[0], wu.at[pl.ds(META, features)], w_sem.at[1]),
        pltpu.make_async_copy(wd_hbm.at[0], wd, w_sem.at[2]),
    ]
    for copy in weight_copies:
        copy.start()
    barrier = pltpu.get_barrier_semaphore()
    neighbours = (x_right, x_left, y_right, y_left, z_right, z_left, sibling)
    for device in neighbours:
        pl.semaphore_signal(barrier, inc=1, device_id=device, device_id_type=MESH)
    tl[0] = blk[...]
    wg[:META, :] = jnp.zeros((META, wg.shape[1]), BF16)
    wu[:META, :] = jnp.zeros((META, wu.shape[1]), BF16)
    pl.semaphore_wait(barrier, len(neighbours))

    def from_left(a):
        return lambda src: remote(src, tr.at[a], tr_s.at[a], tr_r.at[a], z_right)

    def from_right(a):
        return lambda src: remote(src, tl.at[a], tl_s.at[a], tl_r.at[a], z_left)

    from_left(0)(tl.at[0]).start()

    slots = wm.shape[2]
    block = wm.shape[3]
    row = lax.broadcasted_iota(jnp.int32, (slots, block), 0)
    mine = row < slots // 2
    slot = jnp.where(mine, row, row - slots // 2).astype(F32)
    earlier = (
        lax.broadcasted_iota(jnp.int32, (block, block), 0)
        < lax.broadcasted_iota(jnp.int32, (block, block), 1)
    ).astype(F32).astype(BF16)
    expert = loc.astype(F32)
    other = (z * 2 + 1 - core).astype(F32)

    def place(ref, a):
        meta = ref[a, :16, :META].astype(F32)
        ids, weights = meta[:8], meta[8:]
        hit, hit_other = ids == expert, ids == other
        count = lambda v: jnp.sum(v, axis=0, keepdims=True)
        hits = jnp.where(
            mine, count(jnp.where(hit, 1.0, 0.0)), count(jnp.where(hit_other, 1.0, 0.0))
        )
        scale = jnp.where(
            mine, count(jnp.where(hit, weights, 0.0)), count(jnp.where(hit_other, weights, 0.0))
        )
        position = jnp.dot(hits.astype(BF16), earlier, preferred_element_type=F32)
        chosen = jnp.where(position == slot, hits, 0.0)
        rows = jnp.dot(chosen.astype(BF16), ref[a], preferred_element_type=F32).astype(BF16)
        return rows, (chosen * scale).astype(BF16)

    def gather_step(c, j):
        a = c * 2 + j

        @pl.when(a > 0)
        def _():
            from_right(a)(tl.at[0]).wait_recv()

        @pl.when(a < steps - 1)
        def _():
            from_right(a + 1)(tl.at[a]).start()

        from_left(a)(tl.at[0]).wait_recv()

        @pl.when(a < steps - 1)
        def _():
            from_left(a + 1)(tr.at[a]).start()

        half = slots // 2
        for i, ref in enumerate((tr, tl)):
            rows, weights = place(ref, a)
            wm[a, i] = weights
            at = pl.ds(j * slots + i * half, half)
            xb[c, 0, at, :] = rows[:half]
            xs[c, at, :] = rows[half:]

    def x_copy(c):
        return remote(xs.at[c], xb.at[c, 1], x_s.at[c], x_r.at[c], sibling)

    def o_copy(c):
        at = pl.ds(c * 2, 2)
        return remote(os_.at[at], or_.at[at], o_s.at[c], o_r.at[c], sibling)

    sum_a1 = RingSum(
        lambda c, k, i: pa.at[c, k, i], x, x_right, x_left, ra1, sa1, a1_s, a1_r)
    sum_b1 = RingSum(
        lambda c, k, i: pb.at[c, k, i], y, y_right, y_left, rb1, sb1, b1_s, b1_r)
    sum_a2 = RingSum(
        lambda c, k, i: qa.at[c, k, i], y, y_right, y_left, ra2, sa2, a2_s, a2_r)
    sum_b2 = RingSum(
        lambda c, k, i: qb.at[c, k, i], x, x_right, x_left, rb2, sb2, b2_s, b2_r)
    rows_half = lambda ref, c, u, v, h: ref.at[c, u, v, pl.ds(h * 16, 16)]
    gather_a1 = RingGather(
        lambda c, i: ha.at[c, x, i], lambda c, i, h: rows_half(ha, c, x, i, h),
        y, y_right, y_left, ga1_s, ga1_r)
    gather_b1 = RingGather(
        lambda c, i: hb.at[c, y, i], lambda c, i, h: rows_half(hb, c, y, i, h),
        x, x_right, x_left, gb1_s, gb1_r)
    gather_a2 = RingGather(
        lambda c, i: ha.at[c, i], lambda c, i, h: ha.at[c, i, pl.ds(h * 2, 2)],
        x, x_right, x_left, ga2_s, ga2_r)
    gather_b2 = RingGather(
        lambda c, i: hb.at[c, i], lambda c, i, h: hb.at[c, i, pl.ds(h * 2, 2)],
        y, y_right, y_left, gb2_s, gb2_r)

    piece = pa.shape[4]

    def expand(c):
        x_copy(c).wait_recv()
        held = jnp.concatenate([xb[c, 0], xb[c, 1]], axis=0)
        for n in range(SIDE):
            for k, weight in enumerate((wg, wu)):
                part = jnp.dot(
                    held, weight[:, n * 256:(n + 1) * 256], preferred_element_type=F32
                ).astype(BF16)
                for i in range(SIDE):
                    low, lane = (i % 2) * piece, (i // 2) * 128
                    pa[c, k, n, i] = part[low:low + piece, lane:lane + 128]
                    pb[c, k, i, n] = part[2 * piece + low:3 * piece + low, lane:lane + 128]
        sum_a1.first(c)
        sum_b1.first(c)

    def stage2(c):
        sum_a1.second(c)
        sum_b1.second(c)

    def stage3(c):
        for ring, to, then in ((sum_a1, qa, sum_a2), (sum_b1, qb, sum_b2)):
            gate, up = ring.last(c)
            to[c, 0] = gate.astype(BF16)
            to[c, 1] = up.astype(BF16)
            then.first(c)

    def stage4(c):
        sum_a2.second(c)
        sum_b2.second(c)

    def stage5(c):
        gate, up = sum_a2.last(c)
        ha[c, x, y] = (gate / (1.0 + jnp.exp(-gate)) * up).astype(BF16)
        gather_a1.first(c)
        gate, up = sum_b2.last(c)
        hb[c, y, x] = (gate / (1.0 + jnp.exp(-gate)) * up).astype(BF16)
        gather_b1.first(c)

    def stage6(c):
        gather_a1.second(c)
        gather_b1.second(c)

    def stage7(c):
        gather_a1.last(c)
        gather_a2.first(c)
        gather_b1.last(c)
        gather_b2.first(c)

    def stage8(c):
        gather_a2.second(c)
        gather_b2.second(c)

    def contract(c):
        gather_a2.last(c)
        gather_b2.last(c)
        lines = [
            jnp.concatenate([ha[c, u, 2 * v + low] for u in range(SIDE) for v in range(2)], axis=1)
            for low in range(2)
        ] + [
            jnp.concatenate([hb[c, 2 * v + low, u] for u in range(SIDE) for v in range(2)], axis=1)
            for low in range(2)
        ]
        result = jnp.dot(
            jnp.concatenate(lines, axis=0), wd[...], preferred_element_type=F32
        ).astype(BF16)
        for j in range(2):
            for i in range(2):
                low = j * 32 + i * 16
                ob[c * 2 + j, i, :, :features] = result[low:low + 16]
                os_[c * 2 + j, i, :, :features] = result[64 + low:64 + low + 16]
        o_copy(c).start()

    def when(lag, t, stage):
        c = t - lag

        @pl.when(jnp.logical_and(c >= 0, c < chunks))
        def _():
            stage(c)

    def gather_first(c):
        gather_step(c, 0)

    def gather_second(c):
        gather_step(c, 1)
        x_copy(c).start()

    def turn(t, carry):
        when(0, t, gather_first)
        when(2, t, stage2)
        when(3, t, stage3)
        when(4, t, stage4)
        when(5, t, stage5)
        when(0, t, gather_second)

        @pl.when(t == 1)
        def _():
            for copy in weight_copies:
                copy.wait()

        when(1, t, expand)
        when(6, t, stage6)
        when(7, t, stage7)
        when(8, t, stage8)
        when(9, t, contract)
        when(10, t, lambda c: o_copy(c).wait_recv())
        return carry

    lax.fori_loop(0, chunks + 11, turn, 0)

    part = block // 2

    def to_left(a, h):
        return remote(szl.at[a, h], zl.at[a, h], zl_s.at[a, h], zl_r.at[a, h], z_left)

    def to_right(a, h):
        return remote(szr.at[a, h], zr.at[a, h], zr_s.at[a, h], zr_r.at[a, h], z_right)

    def share(a, i):
        held = jnp.concatenate([ob[a, i, :, :features], or_[a, i, :, :features]], axis=0)
        return lax.dot_general(
            wm[a, i], held, (((0,), (0,)), ((), ())), preferred_element_type=F32
        )

    def back(s, carry):
        a = steps - 1 - s
        left_share, right_share = share(a, 0), share(a, 1)
        for h in range(2):
            szl[a, h, :, :features] = left_share[h * part:(h + 1) * part].astype(BF16)

            @pl.when(a < steps - 1)
            def _():
                to_left(a + 1, h).wait_recv()
                szl[a, h, :, :features] = (
                    left_share[h * part:(h + 1) * part] + zl[a + 1, h, :, :features].astype(F32)
                ).astype(BF16)

            to_left(a, h).start()

            @pl.when(a > 0)
            def _():
                szr[a - 1, h, :, :features] = right_share[h * part:(h + 1) * part].astype(BF16)

                @pl.when(a < steps - 1)
                def _():
                    to_right(a, h).wait_recv()
                    szr[a - 1, h, :, :features] = (
                        right_share[h * part:(h + 1) * part] + zr[a, h, :, :features].astype(F32)
                    ).astype(BF16)

                to_right(a - 1, h).start()

        return carry

    lax.fori_loop(0, steps, back, 0)
    own = share(0, 1)
    for h in range(2):
        to_left(0, h).wait_recv()
        to_right(0, h).wait_recv()
        out_ref[h * part:(h + 1) * part, :] = (
            own[h * part:(h + 1) * part]
            + zl[0, h, :, :features].astype(F32)
            + zr[0, h, :, :features].astype(F32)
        ).astype(BF16)

    def finish(c, carry):
        x_copy(c).wait_send()
        o_copy(c).wait_send()
        for ring in (
            sum_a1, sum_b1, sum_a2, sum_b2, gather_a1, gather_b1, gather_a2, gather_b2,
        ):
            ring.finish(c)
        return carry

    lax.fori_loop(0, chunks, finish, 0)

    def finish_z(a, carry):
        from_left(a)(tl.at[0]).wait_send()
        for h in range(2):
            to_left(a, h).wait_send()

        @pl.when(a < steps - 1)
        def _():
            from_right(a + 1)(tl.at[0]).wait_send()
            for h in range(2):
                to_right(a, h).wait_send()

        return carry

    lax.fori_loop(0, steps, finish_z, 0)


def shards(tokens, expert_ids, route_weight, w_gate, w_up, w_down):
    block, features = tokens.shape
    top = expert_ids.shape[1]
    depth = lax.axis_size("loc") // 2
    steps = depth // 2
    chunks = steps // 2
    units = w_gate.shape[2]
    wide = features + META
    meta = jnp.concatenate([expert_ids.astype(BF16).T, route_weight.astype(BF16).T], axis=0)
    meta = jnp.pad(meta, ((0, block - 2 * top), (0, META - block)))
    blk = jnp.concatenate([meta, tokens], axis=1)
    piece = 32
    sem = lambda *shape: pltpu.SemaphoreType.DMA(shape)
    vmem = lambda *shape: pltpu.VMEM(shape, BF16)
    ring = (SIDE, piece, 128)
    scratch = [
        vmem(steps, block, wide), vmem(steps, block, wide),
        vmem(steps, 2, 32, block),
        vmem(chunks, 2, 64, wide), vmem(chunks, 64, wide),
        vmem(wide, units), vmem(wide, units), vmem(units, features),
        vmem(chunks, 2, SIDE, *ring), vmem(chunks, 2, SIDE, *ring),
        vmem(chunks, 6, *ring), vmem(chunks, 2, *ring),
        vmem(chunks, 6, *ring), vmem(chunks, 2, *ring),
        vmem(chunks, 2, *ring), vmem(chunks, 2, *ring),
        vmem(chunks, 6, piece, 128), vmem(chunks, 2, piece, 128),
        vmem(chunks, 6, piece, 128), vmem(chunks, 2, piece, 128),
        vmem(chunks, SIDE, *ring), vmem(chunks, SIDE, *ring),
        vmem(steps, 2, 16, wide), vmem(steps, 2, 16, wide), vmem(steps, 2, 16, wide),
        vmem(steps, 2, block // 2, wide), vmem(steps, 2, block // 2, wide),
        vmem(steps, 2, block // 2, wide), vmem(steps, 2, block // 2, wide),
        sem(3), sem(steps), sem(steps), sem(steps), sem(steps),
        sem(chunks), sem(chunks), sem(chunks), sem(chunks),
    ] + [sem(chunks, 6)] * 8 + [sem(chunks, 4)] * 8 + [sem(steps, 2)] * 4
    rows = chunks * 128
    return pl.pallas_call(
        functools.partial(kernel, steps, chunks),
        out_shape=jax.ShapeDtypeStruct((block, features), BF16),
        in_specs=[pl.BlockSpec(memory_space=pltpu.VMEM)]
        + [pl.BlockSpec(memory_space=pl.ANY)] * 3,
        out_specs=pl.BlockSpec(memory_space=pltpu.VMEM),
        scratch_shapes=scratch,
        compiler_params=pltpu.CompilerParams(
            collective_id=0, has_side_effects=True, vmem_limit_bytes=48 * 1024 * 1024
        ),
        cost_estimate=pl.CostEstimate(
            flops=6 * rows * features * units,
            bytes_accessed=6 * features * units,
            transcendentals=0,
        ),
    )(blk, w_gate, w_up, w_down)


def solution(mesh):
    in_specs = (
        P("loc", "grp"),
        P("loc", None),
        P("loc", None),
        P("loc", "grp", None),
        P("loc", "grp", None),
        P("loc", None, "grp"),
    )
    out_specs = P("loc", "grp")
    return jax.shard_map(shards, mesh=mesh, in_specs=in_specs, out_specs=out_specs, check_vma=False)
```

```python
import functools

import jax
import jax.numpy as jnp
from jax import lax
from jax.experimental import pallas as pl
from jax.experimental.pallas import tpu as pltpu
from jax.sharding import PartitionSpec as P

MESH = pl.DeviceIdType.MESH
BF16 = jnp.bfloat16
F32 = jnp.float32
SIDE = 4
PEERS = (2, 1, 3)
SUBS = 4
META = 64


def remote(src, dst, send_sem, recv_sem, device):
    return pltpu.make_async_remote_copy(
        src_ref=src,
        dst_ref=dst,
        send_sem=send_sem,
        recv_sem=recv_sem,
        device_id=device,
        device_id_type=MESH,
    )


class Scatter:
    def __init__(self, source, place, peers, recv, send_sem, recv_sem):
        self.source, self.place, self.peers, self.recv = source, place, peers, recv
        self.send_sem, self.recv_sem = send_sem, recv_sem

    def copy(self, c, d):
        return remote(
            self.source.at[c, lax.rem(self.place + d, SIDE)], self.recv.at[c, d - 1],
            self.send_sem.at[c, d - 1], self.recv_sem.at[c, d - 1], self.peers[d],
        )

    def start(self, c):
        for d in PEERS:
            self.copy(c, d).start()

    def total(self, c):
        for d in PEERS:
            self.copy(c, d).wait_recv()
        total = self.source[c, self.place].astype(F32)
        for d in PEERS:
            total = total + self.recv[c, d - 1].astype(F32)
        return total

    def finish(self, c):
        for d in PEERS:
            self.copy(c, d).wait_send()


class Gather:
    def __init__(self, piece, place, peers, send_sem, recv_sem):
        self.piece, self.place, self.peers = piece, place, peers
        self.send_sem, self.recv_sem = send_sem, recv_sem

    def copy(self, c, d, back=0):
        ref = self.piece(c, lax.rem(self.place + back, SIDE))
        return remote(
            ref, ref, self.send_sem.at[c, d - 1], self.recv_sem.at[c, d - 1], self.peers[d]
        )

    def start(self, c):
        for d in PEERS:
            self.copy(c, d).start()

    def wait(self, c):
        for d in PEERS:
            self.copy(c, d, SIDE - d).wait_recv()

    def finish(self, c):
        for d in PEERS:
            self.copy(c, d).wait_send()


def kernel(
    chunks, blk, wg_hbm, wu_hbm, wd_hbm, out_ref,
    er, el, odd_r, odd_l, wm, xb, xs, wg, wu, wd,
    pa, pb, ra1, rb1, qa, qb, ra2, rb2, ha, hb, ob, os_, or_,
    szl, zl, szr, zr, sol, zol, sor, zor,
    w_sem, er_s, er_r, el_s, el_r, or_s, or_r, ol_s, ol_r, x_s, x_r, o_s, o_r,
    zl_s, zl_r, zr_s, zr_r, zol_s, zol_r, zor_s, zor_r,
    a1_s, a1_r, b1_s, b1_r, a2_s, a2_r, b2_s, b2_r,
    ga1_s, ga1_r, gb1_s, gb1_r, ga2_s, ga2_r, gb2_s, gb2_r,
):
    features, block = out_ref.shape[1], out_ref.shape[0]
    part, sub = block // 2, block // SUBS
    grp, loc = lax.axis_index("grp"), lax.axis_index("loc")
    depth = lax.axis_size("loc") // 2
    x, y = grp // SIDE, lax.rem(grp, SIDE)
    z, core = loc // 2, lax.rem(loc, 2)
    x_peers = [(lax.rem(x + d, SIDE) * SIDE + y, loc) for d in range(SIDE)]
    y_peers = [(x * SIDE + lax.rem(y + d, SIDE), loc) for d in range(SIDE)]
    z_right, z_right2, z_left, z_left2 = (
        (grp, lax.rem(z + d, depth) * 2 + core) for d in (1, 2, depth - 1, depth - 2)
    )
    sibling = (grp, z * 2 + 1 - core)

    weight_copies = [
        pltpu.make_async_copy(wg_hbm.at[0], wg.at[pl.ds(META, features)], w_sem.at[0]),
        pltpu.make_async_copy(wu_hbm.at[0], wu.at[pl.ds(META, features)], w_sem.at[1]),
        pltpu.make_async_copy(wd_hbm.at[0], wd, w_sem.at[2]),
    ]
    barrier = pltpu.get_barrier_semaphore()
    neighbours = x_peers[1:] + y_peers[1:] + [z_right, z_right2, z_left, z_left2, sibling]
    for device in neighbours:
        pl.semaphore_signal(barrier, inc=1, device_id=device, device_id_type=MESH)
    el[0] = blk[...]
    wg[:META, :] = jnp.zeros((META, wg.shape[1]), BF16)
    wu[:META, :] = jnp.zeros((META, wu.shape[1]), BF16)
    for copy in weight_copies:
        copy.start()
    pl.semaphore_wait(barrier, len(neighbours))

    def half(ref, k, h):
        return ref.at[k, pl.ds(h * part, part)]

    def even_right(k, h, ref, j):
        return remote(half(ref, j, h), half(er, k, h), er_s.at[k, h], er_r.at[k, h], z_right2)

    def even_left(k, h, ref, j):
        return remote(half(ref, j, h), half(el, k, h), el_s.at[k, h], el_r.at[k, h], z_left2)

    def odd_right(k, ref, j):
        return remote(ref.at[j], odd_r.at[k], or_s.at[k], or_r.at[k], z_right)

    def odd_left(k, ref, j):
        return remote(ref.at[j], odd_l.at[k], ol_s.at[k], ol_r.at[k], z_left)

    for h in range(2):
        even_right(0, h, el, 0).start()
        even_left(1, h, el, 0).start()
    odd_right(0, el, 0).start()
    odd_left(0, el, 0).start()

    slots = wm.shape[2]
    row = lax.broadcasted_iota(jnp.int32, (slots, block), 0)
    mine = row < slots // 2
    slot = jnp.where(mine, row, row - slots // 2).astype(F32)
    earlier = (
        lax.broadcasted_iota(jnp.int32, (block, block), 0)
        < lax.broadcasted_iota(jnp.int32, (block, block), 1)
    ).astype(F32).astype(BF16)
    expert = loc.astype(F32)
    other = (z * 2 + 1 - core).astype(F32)

    def place(ref, k):
        meta = ref[k, :16, :META].astype(F32)
        ids, weights = meta[:8], meta[8:]
        hit, hit_other = ids == expert, ids == other
        count = lambda v: jnp.sum(v, axis=0, keepdims=True)
        hits = jnp.where(
            mine, count(jnp.where(hit, 1.0, 0.0)), count(jnp.where(hit_other, 1.0, 0.0))
        )
        scale = jnp.where(
            mine, count(jnp.where(hit, weights, 0.0)), count(jnp.where(hit_other, weights, 0.0))
        )
        position = jnp.dot(hits.astype(BF16), earlier, preferred_element_type=F32)
        chosen = jnp.where(position == slot, hits, 0.0)
        rows = jnp.dot(chosen.astype(BF16), ref[k], preferred_element_type=F32).astype(BF16)
        return rows, (chosen * scale).astype(BF16)

    def x_copy(c):
        return remote(xs.at[c], xb.at[c, 1], x_s.at[c], x_r.at[c], sibling)

    def o_copy(c):
        return remote(os_.at[c], or_.at[c], o_s.at[c], o_r.at[c], sibling)

    def gather_step(k):
        for h in range(2):
            even_right(k, h, el, 0).wait_recv()

            @pl.when(k < chunks - 1)
            def _():
                even_right(k + 1, h, er, k).start()

            @pl.when(k > 0)
            def _():
                even_left(k, h, el, 0).wait_recv()

            @pl.when(jnp.logical_and(k > 0, k < chunks - 1))
            def _():
                even_left(k + 1, h, el, k).start()

        @pl.when(k < chunks - 1)
        def _():
            odd_right(k + 1, er, k).start()

        @pl.when(k > 0)
        def _():
            odd_left(k, el, k).start()

    def place_all(k):
        odd_right(k, el, 0).wait_recv()
        odd_left(k, el, 0).wait_recv()
        got = [place(ref, k) for ref in (er, el, odd_r, odd_l)]
        for i, (rows, weights) in enumerate(got):
            wm[k, i] = weights
            xb[k, 0, i * 16:(i + 1) * 16, :] = rows[:16]
            xs[k, i * 16:(i + 1) * 16, :] = rows[16:]
        x_copy(k).start()

    sum_a1 = Scatter(pa, x, x_peers, ra1, a1_s, a1_r)
    sum_b1 = Scatter(pb, y, y_peers, rb1, b1_s, b1_r)
    sum_a2 = Scatter(qa, y, y_peers, ra2, a2_s, a2_r)
    sum_b2 = Scatter(qb, x, x_peers, rb2, b2_s, b2_r)
    gather_a1 = Gather(lambda c, i: ha.at[c, x, i], y, y_peers, ga1_s, ga1_r)
    gather_b1 = Gather(lambda c, i: hb.at[c, y, i], x, x_peers, gb1_s, gb1_r)
    gather_a2 = Gather(lambda c, i: ha.at[c, i], x, x_peers, ga2_s, ga2_r)
    gather_b2 = Gather(lambda c, i: hb.at[c, i], y, y_peers, gb2_s, gb2_r)
    piece = pa.shape[4]

    def expand(c):
        x_copy(c).wait_recv()
        held = jnp.concatenate([xb[c, 0], xb[c, 1]], axis=0)
        for n in range(SIDE):
            for k, weight in enumerate((wg, wu)):
                term = jnp.dot(
                    held, weight[:, n * 256:(n + 1) * 256], preferred_element_type=F32
                ).astype(BF16)
                for i in range(SIDE):
                    low, lane = (i % 2) * piece, (i // 2) * 128
                    pa[c, n, k, i] = term[low:low + piece, lane:lane + 128]
                    pb[c, i, k, n] = term[2 * piece + low:3 * piece + low, lane:lane + 128]
        sum_a1.start(c)
        sum_b1.start(c)

    def stage2(c):
        for ring, to, then in ((sum_a1, qa, sum_a2), (sum_b1, qb, sum_b2)):
            total = ring.total(c).astype(BF16)
            for i in range(SIDE):
                to[c, i] = total[:, i]
            then.start(c)

    def stage3(c):
        total = sum_a2.total(c)
        ha[c, x, y] = (total[0] / (1.0 + jnp.exp(-total[0])) * total[1]).astype(BF16)
        gather_a1.start(c)
        total = sum_b2.total(c)
        hb[c, y, x] = (total[0] / (1.0 + jnp.exp(-total[0])) * total[1]).astype(BF16)
        gather_b1.start(c)

    def stage4(c):
        gather_a1.wait(c)
        gather_a2.start(c)
        gather_b1.wait(c)
        gather_b2.start(c)

    def contract(c):
        gather_a2.wait(c)
        gather_b2.wait(c)
        lines = [
            jnp.concatenate([ha[c, u, 2 * v + low] for u in range(SIDE) for v in range(2)], axis=1)
            for low in range(2)
        ] + [
            jnp.concatenate([hb[c, 2 * v + low, u] for u in range(SIDE) for v in range(2)], axis=1)
            for low in range(2)
        ]
        result = lax.dot_general(
            jnp.concatenate(lines, axis=0), wd[...], (((1,), (1,)), ((), ())),
            preferred_element_type=F32,
        ).astype(BF16)
        for i in range(4):
            ob[c, i, :, :features] = result[i * 16:(i + 1) * 16]
            os_[c, i, :, :features] = result[64 + i * 16:64 + (i + 1) * 16]
        o_copy(c).start()

    def to_left2(k, h):
        return remote(szl.at[k, h], zl.at[k, h], zl_s.at[k, h], zl_r.at[k, h], z_left2)

    def to_right2(k, h):
        return remote(szr.at[k, h], zr.at[k, h], zr_s.at[k, h], zr_r.at[k, h], z_right2)

    def to_left(k):
        return remote(sol.at[k], zol.at[k], zol_s.at[k], zol_r.at[k], z_left)

    def to_right(k):
        return remote(sor.at[k], zor.at[k], zor_s.at[k], zor_r.at[k], z_right)

    def share(k, i):
        held = jnp.concatenate([ob[k, i, :, :features], or_[k, i, :, :features]], axis=0)
        return lax.dot_general(
            wm[k, i], held, (((0,), (0,)), ((), ())), preferred_element_type=F32
        )

    def odd_shares(c):
        o_copy(c).wait_recv()
        sol[c, :, :features] = share(c, 2).astype(BF16)
        to_left(c).start()
        sor[c, :, :features] = share(c, 3).astype(BF16)
        to_right(c).start()

    def when(lag, t, stage):
        c = t - lag

        @pl.when(jnp.logical_and(c >= 0, c < chunks))
        def _():
            stage(c)

    def turn(t, carry):
        when(0, t, gather_step)

        @pl.when(t == 0)
        def _():
            for copy in weight_copies:
                copy.wait()

        when(1, t, place_all)
        when(2, t, stage2)
        when(1, t, expand)
        when(3, t, stage3)
        when(4, t, stage4)
        when(6, t, odd_shares)
        when(5, t, contract)
        return carry

    lax.fori_loop(0, chunks + 6, turn, 0)

    def back(k, first=False, last=False):
        left_share = share(k, 0)
        if not first:
            to_left(k + 1).wait_recv()
        if not last:
            right_share = share(k, 1)
            to_right(k).wait_recv()
        for h in range(SUBS):
            rows = slice(h * sub, (h + 1) * sub)
            total = left_share[rows]
            if not first:
                total = total + zol[k + 1, rows, :features].astype(F32)
                to_left2(k + 1, h).wait_recv()
                total = total + zl[k + 1, h, :, :features].astype(F32)
            szl[k, h, :, :features] = total.astype(BF16)
            to_left2(k, h).start()
            if not last:
                total = right_share[rows] + zor[k, rows, :features].astype(F32)
                if not first:
                    to_right2(k + 1, h).wait_recv()
                    total = total + zr[k + 1, h, :, :features].astype(F32)
                szr[k, h, :, :features] = total.astype(BF16)
                to_right2(k, h).start()

    def back_turn(i, carry):
        back(chunks - 2 - i)
        return carry

    back(chunks - 1, first=True)
    lax.fori_loop(0, chunks - 2, back_turn, 0)
    back(0, last=True)
    own = share(0, 1)
    to_left(0).wait_recv()
    to_right(0).wait_recv()
    for h in range(SUBS):
        rows = slice(h * sub, (h + 1) * sub)
        to_left2(0, h).wait_recv()
        to_right2(1, h).wait_recv()
        out_ref[rows, :] = (
            own[rows]
            + zol[0, rows, :features].astype(F32)
            + zor[0, rows, :features].astype(F32)
            + zl[0, h, :, :features].astype(F32)
            + zr[1, h, :, :features].astype(F32)
        ).astype(BF16)

    def finish(k, carry):
        x_copy(k).wait_send()
        o_copy(k).wait_send()
        for stage in (
            sum_a1, sum_b1, sum_a2, sum_b2, gather_a1, gather_b1, gather_a2, gather_b2,
        ):
            stage.finish(k)
        odd_right(k, el, 0).wait_send()
        odd_left(k, el, 0).wait_send()
        to_left(k).wait_send()
        to_right(k).wait_send()
        for h in range(2):
            even_right(k, h, el, 0).wait_send()
        for h in range(SUBS):
            to_left2(k, h).wait_send()

        @pl.when(k > 0)
        def _():
            for h in range(2):
                even_left(k, h, el, 0).wait_send()
            for h in range(SUBS):
                to_right2(k, h).wait_send()

        return carry

    lax.fori_loop(0, chunks, finish, 0)


def shards(tokens, expert_ids, route_weight, w_gate, w_up, w_down):
    block, features = tokens.shape
    top = expert_ids.shape[1]
    chunks = lax.axis_size("loc") // 8
    units = w_gate.shape[2]
    wide = features + META
    meta = jnp.concatenate([expert_ids.astype(BF16).T, route_weight.astype(BF16).T], axis=0)
    meta = jnp.pad(meta, ((0, block - 2 * top), (0, META - block)))
    blk = jnp.concatenate([meta, tokens], axis=1)
    piece = 32
    sem = lambda *shape: pltpu.SemaphoreType.DMA(shape)
    vmem = lambda *shape: pltpu.VMEM(shape, BF16)
    ring = (SIDE, piece, 128)
    blocks = (chunks, block, wide)
    subs = (chunks, SUBS, block // SUBS, wide)
    scratch = (
        [vmem(*blocks)] * 4
        + [vmem(chunks, 4, 32, block), vmem(chunks, 2, 64, wide), vmem(chunks, 64, wide)]
        + [vmem(wide, units), vmem(wide, units), vmem(features, units)]
        + [vmem(chunks, SIDE, 2, *ring)] * 2
        + [vmem(chunks, 3, 2, *ring)] * 2
        + [vmem(chunks, SIDE, 2, piece, 128)] * 2
        + [vmem(chunks, 3, 2, piece, 128)] * 2
        + [vmem(chunks, SIDE, *ring)] * 2
        + [vmem(chunks, 4, 16, wide)] * 3
        + [vmem(*subs)] * 4
        + [vmem(*blocks)] * 4
        + [sem(3)]
        + [sem(chunks, 2)] * 4
        + [sem(chunks)] * 8
        + [sem(chunks, SUBS)] * 4
        + [sem(chunks)] * 4
        + [sem(chunks, 3)] * 16
    )
    rows = chunks * 128
    return pl.pallas_call(
        functools.partial(kernel, chunks),
        out_shape=jax.ShapeDtypeStruct((block, features), BF16),
        in_specs=[pl.BlockSpec(memory_space=pltpu.VMEM)]
        + [pl.BlockSpec(memory_space=pl.ANY)] * 3,
        out_specs=pl.BlockSpec(memory_space=pltpu.VMEM),
        scratch_shapes=scratch,
        compiler_params=pltpu.CompilerParams(
            collective_id=0, has_side_effects=True, vmem_limit_bytes=48 * 1024 * 1024
        ),
        cost_estimate=pl.CostEstimate(
            flops=6 * rows * features * units,
            bytes_accessed=6 * features * units,
            transcendentals=0,
        ),
    )(blk, w_gate, w_up, jnp.swapaxes(w_down, 1, 2))


def solution(mesh):
    in_specs = (
        P("loc", "grp"),
        P("loc", None),
        P("loc", None),
        P("loc", "grp", None),
        P("loc", "grp", None),
        P("loc", None, "grp"),
    )
    out_specs = P("loc", "grp")
    return jax.shard_map(shards, mesh=mesh, in_specs=in_specs, out_specs=out_specs, check_vma=False)
```

```python
import functools

import jax
import jax.numpy as jnp
from jax import lax
from jax.experimental import pallas as pl
from jax.experimental.pallas import tpu as pltpu
from jax.sharding import PartitionSpec as P

MESH = pl.DeviceIdType.MESH
BF16 = jnp.bfloat16
F32 = jnp.float32
SIDE = 4
PEERS = (2, 1, 3)
SUBS = 4
META = 64


def remote(src, dst, send_sem, recv_sem, device):
    return pltpu.make_async_remote_copy(
        src_ref=src,
        dst_ref=dst,
        send_sem=send_sem,
        recv_sem=recv_sem,
        device_id=device,
        device_id_type=MESH,
    )


class Scatter:
    def __init__(self, source, place, peers, recv, send_sem, recv_sem):
        self.source, self.place, self.peers, self.recv = source, place, peers, recv
        self.send_sem, self.recv_sem = send_sem, recv_sem

    def copy(self, c, d):
        return remote(
            self.source.at[c, lax.rem(self.place + d, SIDE)], self.recv.at[c, d - 1],
            self.send_sem.at[c, d - 1], self.recv_sem.at[c, d - 1], self.peers[d],
        )

    def start(self, c):
        for d in PEERS:
            self.copy(c, d).start()

    def total(self, c):
        for d in PEERS:
            self.copy(c, d).wait_recv()
        total = self.source[c, self.place].astype(F32)
        for d in PEERS:
            total = total + self.recv[c, d - 1].astype(F32)
        return total

    def finish(self, c):
        for d in PEERS:
            self.copy(c, d).wait_send()


class Gather:
    def __init__(self, piece, place, peers, send_sem, recv_sem):
        self.piece, self.place, self.peers = piece, place, peers
        self.send_sem, self.recv_sem = send_sem, recv_sem

    def copy(self, c, d, back=0):
        ref = self.piece(c, lax.rem(self.place + back, SIDE))
        return remote(
            ref, ref, self.send_sem.at[c, d - 1], self.recv_sem.at[c, d - 1], self.peers[d]
        )

    def start(self, c):
        for d in PEERS:
            self.copy(c, d).start()

    def wait(self, c):
        for d in PEERS:
            self.copy(c, d, SIDE - d).wait_recv()

    def finish(self, c):
        for d in PEERS:
            self.copy(c, d).wait_send()


def kernel(
    chunks, tokens, ids_t, weights_t, wg_hbm, wu_hbm, wd_hbm, out_ref,
    er, el, odd_r, odd_l, wm, xb, xs, wg, wu, wd,
    pa, pb, ra1, rb1, qa, qb, ra2, rb2, ha, hb, ob, os_, or_,
    szl, zl, szr, zr, sol, zol, sor, zor,
    w_sem, er_s, er_r, el_s, el_r, or_s, or_r, ol_s, ol_r, x_s, x_r, o_s, o_r,
    zl_s, zl_r, zr_s, zr_r, zol_s, zol_r, zor_s, zor_r,
    a1_s, a1_r, b1_s, b1_r, a2_s, a2_r, b2_s, b2_r,
    ga1_s, ga1_r, gb1_s, gb1_r, ga2_s, ga2_r, gb2_s, gb2_r,
):
    features, block = out_ref.shape[1], out_ref.shape[0]
    part, sub = block // 2, block // SUBS
    grp, loc = lax.axis_index("grp"), lax.axis_index("loc")
    depth = lax.axis_size("loc") // 2
    x, y = grp // SIDE, lax.rem(grp, SIDE)
    z, core = loc // 2, lax.rem(loc, 2)
    x_peers = [(lax.rem(x + d, SIDE) * SIDE + y, loc) for d in range(SIDE)]
    y_peers = [(x * SIDE + lax.rem(y + d, SIDE), loc) for d in range(SIDE)]
    z_right, z_right2, z_left, z_left2 = (
        (grp, lax.rem(z + d, depth) * 2 + core) for d in (1, 2, depth - 1, depth - 2)
    )
    sibling = (grp, z * 2 + 1 - core)

    weight_copies = [
        pltpu.make_async_copy(wg_hbm.at[0], wg.at[pl.ds(META, features)], w_sem.at[0]),
        pltpu.make_async_copy(wu_hbm.at[0], wu.at[pl.ds(META, features)], w_sem.at[1]),
        pltpu.make_async_copy(wd_hbm.at[0], wd, w_sem.at[2]),
    ]
    barrier = pltpu.get_barrier_semaphore()
    neighbours = x_peers[1:] + y_peers[1:] + [z_right, z_right2, z_left, z_left2, sibling]
    for device in neighbours:
        pl.semaphore_signal(barrier, inc=1, device_id=device, device_id_type=MESH)
    el[0, :, META:] = tokens[...]
    el[0, 16:, :META] = jnp.zeros((block - 16, META), BF16)
    el[0, :16, :META] = jnp.concatenate(
        [ids_t[...].astype(F32), weights_t[...]], axis=0
    ).astype(BF16)
    wg[:META, :] = jnp.zeros((META, wg.shape[1]), BF16)
    wu[:META, :] = jnp.zeros((META, wu.shape[1]), BF16)
    for copy in weight_copies:
        copy.start()
    pl.semaphore_wait(barrier, len(neighbours))

    def half(ref, k, h):
        return ref.at[k, pl.ds(h * part, part)]

    def even_right(k, h, ref, j):
        return remote(half(ref, j, h), half(er, k, h), er_s.at[k, h], er_r.at[k, h], z_right2)

    def even_left(k, h, ref, j):
        return remote(half(ref, j, h), half(el, k, h), el_s.at[k, h], el_r.at[k, h], z_left2)

    def odd_right(k, ref, j):
        return remote(ref.at[j], odd_r.at[k], or_s.at[k], or_r.at[k], z_right)

    def odd_left(k, ref, j):
        return remote(ref.at[j], odd_l.at[k], ol_s.at[k], ol_r.at[k], z_left)

    for h in range(2):
        even_right(0, h, el, 0).start()
        even_left(1, h, el, 0).start()
    odd_right(0, el, 0).start()
    odd_left(0, el, 0).start()

    slots = wm.shape[2]
    row = lax.broadcasted_iota(jnp.int32, (slots, block), 0)
    mine = row < slots // 2
    slot = jnp.where(mine, row, row - slots // 2).astype(F32)
    earlier = (
        lax.broadcasted_iota(jnp.int32, (block, block), 0)
        < lax.broadcasted_iota(jnp.int32, (block, block), 1)
    ).astype(F32).astype(BF16)
    expert = loc.astype(F32)
    other = (z * 2 + 1 - core).astype(F32)

    def place(ref, k):
        meta = ref[k, :16, :META].astype(F32)
        ids, weights = meta[:8], meta[8:]
        hit, hit_other = ids == expert, ids == other
        count = lambda v: jnp.sum(v, axis=0, keepdims=True)
        hits = jnp.where(
            mine, count(jnp.where(hit, 1.0, 0.0)), count(jnp.where(hit_other, 1.0, 0.0))
        )
        scale = jnp.where(
            mine, count(jnp.where(hit, weights, 0.0)), count(jnp.where(hit_other, weights, 0.0))
        )
        position = jnp.dot(hits.astype(BF16), earlier, preferred_element_type=F32)
        chosen = jnp.where(position == slot, hits, 0.0)
        rows = jnp.dot(chosen.astype(BF16), ref[k], preferred_element_type=F32).astype(BF16)
        return rows, (chosen * scale).astype(BF16)

    def x_copy(c):
        return remote(xs.at[c], xb.at[c, 1], x_s.at[c], x_r.at[c], sibling)

    def o_copy(c):
        return remote(os_.at[c], or_.at[c], o_s.at[c], o_r.at[c], sibling)

    def gather_step(k):
        for h in range(2):
            even_right(k, h, el, 0).wait_recv()

            @pl.when(k < chunks - 1)
            def _():
                even_right(k + 1, h, er, k).start()

            @pl.when(k > 0)
            def _():
                even_left(k, h, el, 0).wait_recv()

            @pl.when(jnp.logical_and(k > 0, k < chunks - 1))
            def _():
                even_left(k + 1, h, el, k).start()

        @pl.when(k < chunks - 1)
        def _():
            odd_right(k + 1, er, k).start()

        @pl.when(k > 0)
        def _():
            odd_left(k, el, k).start()

    def place_all(k):
        odd_right(k, el, 0).wait_recv()
        odd_left(k, el, 0).wait_recv()
        got = [place(ref, k) for ref in (er, el, odd_r, odd_l)]
        for i, (rows, weights) in enumerate(got):
            wm[k, i] = weights
            xb[k, 0, i * 16:(i + 1) * 16, :] = rows[:16]
            xs[k, i * 16:(i + 1) * 16, :] = rows[16:]
        x_copy(k).start()

    sum_a1 = Scatter(pa, x, x_peers, ra1, a1_s, a1_r)
    sum_b1 = Scatter(pb, y, y_peers, rb1, b1_s, b1_r)
    sum_a2 = Scatter(qa, y, y_peers, ra2, a2_s, a2_r)
    sum_b2 = Scatter(qb, x, x_peers, rb2, b2_s, b2_r)
    gather_a1 = Gather(lambda c, i: ha.at[c, x, i], y, y_peers, ga1_s, ga1_r)
    gather_b1 = Gather(lambda c, i: hb.at[c, y, i], x, x_peers, gb1_s, gb1_r)
    gather_a2 = Gather(lambda c, i: ha.at[c, i], x, x_peers, ga2_s, ga2_r)
    gather_b2 = Gather(lambda c, i: hb.at[c, i], y, y_peers, gb2_s, gb2_r)
    piece = pa.shape[4]

    def expand(c):
        x_copy(c).wait_recv()
        held = jnp.concatenate([xb[c, 0], xb[c, 1]], axis=0)
        for n in range(SIDE):
            for k, weight in enumerate((wg, wu)):
                term = jnp.dot(
                    held, weight[:, n * 256:(n + 1) * 256], preferred_element_type=F32
                ).astype(BF16)
                for i in range(SIDE):
                    low, lane = (i % 2) * piece, (i // 2) * 128
                    pa[c, n, k, i] = term[low:low + piece, lane:lane + 128]
                    pb[c, i, k, n] = term[2 * piece + low:3 * piece + low, lane:lane + 128]
        sum_a1.start(c)
        sum_b1.start(c)

    def stage2(c):
        for ring, to, then in ((sum_a1, qa, sum_a2), (sum_b1, qb, sum_b2)):
            total = ring.total(c).astype(BF16)
            for i in range(SIDE):
                to[c, i] = total[:, i]
            then.start(c)

    def stage3(c):
        total = sum_a2.total(c)
        ha[c, x, y] = (total[0] / (1.0 + jnp.exp(-total[0])) * total[1]).astype(BF16)
        gather_a1.start(c)
        total = sum_b2.total(c)
        hb[c, y, x] = (total[0] / (1.0 + jnp.exp(-total[0])) * total[1]).astype(BF16)
        gather_b1.start(c)

    def stage4(c):
        gather_a1.wait(c)
        gather_a2.start(c)
        gather_b1.wait(c)
        gather_b2.start(c)

    def contract(c):
        gather_a2.wait(c)
        gather_b2.wait(c)
        lines = [
            jnp.concatenate([ha[c, u, 2 * v + low] for u in range(SIDE) for v in range(2)], axis=1)
            for low in range(2)
        ] + [
            jnp.concatenate([hb[c, 2 * v + low, u] for u in range(SIDE) for v in range(2)], axis=1)
            for low in range(2)
        ]
        result = lax.dot_general(
            jnp.concatenate(lines, axis=0), wd[...], (((1,), (1,)), ((), ())),
            preferred_element_type=F32,
        ).astype(BF16)
        for i in range(4):
            ob[c, i, :, :features] = result[i * 16:(i + 1) * 16]
            os_[c, i, :, :features] = result[64 + i * 16:64 + (i + 1) * 16]
        o_copy(c).start()

    def to_left2(k, h):
        return remote(szl.at[k, h], zl.at[k, h], zl_s.at[k, h], zl_r.at[k, h], z_left2)

    def to_right2(k, h):
        return remote(szr.at[k, h], zr.at[k, h], zr_s.at[k, h], zr_r.at[k, h], z_right2)

    def to_left(k):
        return remote(sol.at[k], zol.at[k], zol_s.at[k], zol_r.at[k], z_left)

    def to_right(k):
        return remote(sor.at[k], zor.at[k], zor_s.at[k], zor_r.at[k], z_right)

    def share(k, i):
        held = jnp.concatenate([ob[k, i, :, :features], or_[k, i, :, :features]], axis=0)
        return lax.dot_general(
            wm[k, i], held, (((0,), (0,)), ((), ())), preferred_element_type=F32
        )

    def odd_shares(c):
        o_copy(c).wait_recv()
        sol[c, :, :features] = share(c, 2).astype(BF16)
        to_left(c).start()
        sor[c, :, :features] = share(c, 3).astype(BF16)
        to_right(c).start()

    def when(lag, t, stage):
        c = t - lag

        @pl.when(jnp.logical_and(c >= 0, c < chunks))
        def _():
            stage(c)

    def turn(t, carry):
        when(0, t, gather_step)

        @pl.when(t == 0)
        def _():
            for copy in weight_copies:
                copy.wait()

        when(1, t, place_all)
        when(2, t, stage2)
        when(1, t, expand)
        when(3, t, stage3)
        when(4, t, stage4)
        when(6, t, odd_shares)
        when(5, t, contract)
        return carry

    lax.fori_loop(0, chunks + 6, turn, 0)

    def back(k, first=False, last=False):
        left_share = share(k, 0)
        if not first:
            to_left(k + 1).wait_recv()
        if not last:
            right_share = share(k, 1)
            to_right(k).wait_recv()
        for h in range(SUBS):
            rows = slice(h * sub, (h + 1) * sub)
            total = left_share[rows]
            if not first:
                total = total + zol[k + 1, rows, :features].astype(F32)
                to_left2(k + 1, h).wait_recv()
                total = total + zl[k + 1, h, :, :features].astype(F32)
            szl[k, h, :, :features] = total.astype(BF16)
            to_left2(k, h).start()
            if not last:
                total = right_share[rows] + zor[k, rows, :features].astype(F32)
                if not first:
                    to_right2(k + 1, h).wait_recv()
                    total = total + zr[k + 1, h, :, :features].astype(F32)
                szr[k, h, :, :features] = total.astype(BF16)
                to_right2(k, h).start()

    def back_turn(i, carry):
        back(chunks - 2 - i)
        return carry

    back(chunks - 1, first=True)
    lax.fori_loop(0, chunks - 2, back_turn, 0)
    back(0, last=True)
    own = share(0, 1)
    to_left(0).wait_recv()
    to_right(0).wait_recv()
    for h in range(SUBS):
        rows = slice(h * sub, (h + 1) * sub)
        to_left2(0, h).wait_recv()
        to_right2(1, h).wait_recv()
        out_ref[rows, :] = (
            own[rows]
            + zol[0, rows, :features].astype(F32)
            + zor[0, rows, :features].astype(F32)
            + zl[0, h, :, :features].astype(F32)
            + zr[1, h, :, :features].astype(F32)
        ).astype(BF16)

    def finish(k, carry):
        x_copy(k).wait_send()
        o_copy(k).wait_send()
        for stage in (
            sum_a1, sum_b1, sum_a2, sum_b2, gather_a1, gather_b1, gather_a2, gather_b2,
        ):
            stage.finish(k)
        odd_right(k, el, 0).wait_send()
        odd_left(k, el, 0).wait_send()
        to_left(k).wait_send()
        to_right(k).wait_send()
        for h in range(2):
            even_right(k, h, el, 0).wait_send()
        for h in range(SUBS):
            to_left2(k, h).wait_send()

        @pl.when(k > 0)
        def _():
            for h in range(2):
                even_left(k, h, el, 0).wait_send()
            for h in range(SUBS):
                to_right2(k, h).wait_send()

        return carry

    lax.fori_loop(0, chunks, finish, 0)


def shards(tokens, expert_ids, route_weight, w_gate, w_up, w_down):
    block, features = tokens.shape
    chunks = lax.axis_size("loc") // 8
    units = w_gate.shape[2]
    wide = features + META
    piece = 32
    sem = lambda *shape: pltpu.SemaphoreType.DMA(shape)
    vmem = lambda *shape: pltpu.VMEM(shape, BF16)
    ring = (SIDE, piece, 128)
    blocks = (chunks, block, wide)
    subs = (chunks, SUBS, block // SUBS, wide)
    scratch = (
        [vmem(*blocks)] * 4
        + [vmem(chunks, 4, 32, block), vmem(chunks, 2, 64, wide), vmem(chunks, 64, wide)]
        + [vmem(wide, units), vmem(wide, units), vmem(features, units)]
        + [vmem(chunks, SIDE, 2, *ring)] * 2
        + [vmem(chunks, 3, 2, *ring)] * 2
        + [vmem(chunks, SIDE, 2, piece, 128)] * 2
        + [vmem(chunks, 3, 2, piece, 128)] * 2
        + [vmem(chunks, SIDE, *ring)] * 2
        + [vmem(chunks, 4, 16, wide)] * 3
        + [vmem(*subs)] * 4
        + [vmem(*blocks)] * 4
        + [sem(3)]
        + [sem(chunks, 2)] * 4
        + [sem(chunks)] * 8
        + [sem(chunks, SUBS)] * 4
        + [sem(chunks)] * 4
        + [sem(chunks, 3)] * 16
    )
    rows = chunks * 128
    return pl.pallas_call(
        functools.partial(kernel, chunks),
        out_shape=jax.ShapeDtypeStruct((block, features), BF16),
        in_specs=[pl.BlockSpec(memory_space=pltpu.VMEM)] * 3
        + [pl.BlockSpec(memory_space=pltpu.HBM)] * 3,
        out_specs=pl.BlockSpec(memory_space=pltpu.VMEM),
        scratch_shapes=scratch,
        compiler_params=pltpu.CompilerParams(
            collective_id=0, has_side_effects=True, vmem_limit_bytes=60 * 1024 * 1024
        ),
        cost_estimate=pl.CostEstimate(
            flops=6 * rows * features * units,
            bytes_accessed=6 * features * units,
            transcendentals=0,
        ),
    )(tokens, expert_ids.T, route_weight.T, w_gate, w_up, jnp.swapaxes(w_down, 1, 2))


def solution(mesh):
    in_specs = (
        P("loc", "grp"),
        P("loc", None),
        P("loc", None),
        P("loc", "grp", None),
        P("loc", "grp", None),
        P("loc", None, "grp"),
    )
    out_specs = P("loc", "grp")
    return jax.shard_map(shards, mesh=mesh, in_specs=in_specs, out_specs=out_specs, check_vma=False)
```
